128 devices in a mesh: row: 128 (over y, x, z, core).
Axes of the slice: x: 4, y: 4, z: 4, core: 2. Of those that a mesh axis runs over, the one named last changes fastest.
Arguments:
- matrix_blocks: bfloat16 [256, 48, 256, 256], P('row'), may hold values from -0.078125 to 0.078125
- test_panel: bfloat16 [65536, 256], P('row'), may hold values from -6 to 6
- column_blocks: int32 [256, 48], P('row'), may hold values from 0 to 255, as said below
- row_counts: int32 [256], P('row'), may hold values from 16 to 48, as said below
Outputs:
- basis: float32 [65536, 256], P('row')
- triangle: float32 [256, 256], replicated
The draws below stay inside these ranges and needn't reach their ends.
Inputs may be any that keep to these rules, and one draw needn't show every extreme that they name: `column_blocks`: block column indices of all slots, padding slots too. Among the slots of the 2 block rows of one device, at most 1 have a column block in the 2 block rows held by any one device (block c is held by device c // 2), and the first slot of each device's first block row is always live (every row has at least 16 live slots). `row_counts`: live slots per block row; some block row is full.
All inputs are finite; a program needn't handle non-finite values.
Results may differ from the reference program's by a relative error of at most 0.0003.
Values may be sent and summed in bfloat16 or wider, within the bound.
A program may use at most 192 MiB of HBM per device.

```python
import math
import jax
import jax.numpy as jnp
from jax import lax

BS = 256
K = 256
MAXB = 48
MINB = 16
R_DEV = 2
NB = 256
CAP = 1


def draw_column_blocks(key, part):
    key = jax.random.fold_in(key, 11)
    holders = NB // R_DEV
    slot_total = R_DEV * MAXB
    pool_size = holders * CAP

    def one_holder(sub_key):
        first_key, second_key, third_key = jax.random.split(sub_key, 3)
        base = jnp.arange(pool_size, dtype=jnp.int32) // CAP
        shuffled = jax.random.permutation(first_key, base[CAP:])
        ordered = jnp.concatenate([base[:CAP], shuffled])[:slot_total]
        relabel = jax.random.permutation(second_key, jnp.arange(holders, dtype=jnp.int32))
        owners = relabel[ordered]
        within = jax.random.randint(third_key, (slot_total,), 0, R_DEV, dtype=jnp.int32)
        return (owners * R_DEV + within).reshape(R_DEV, MAXB)
    holder_keys = jax.random.split(key, holders)
    return jax.vmap(one_holder)(holder_keys).reshape(NB, MAXB).astype(jnp.int32)


def draw_row_counts(key, part):
    key = jax.random.fold_in(key, 23)
    holders = NB // R_DEV
    first_key, second_key, third_key = jax.random.split(key, 3)
    level = jax.random.randint(first_key, (holders, 1), 0, 4, dtype=jnp.int32)
    spread = (MAXB - MINB) * (level + 2) // 5
    extra = jax.random.randint(second_key, (holders, R_DEV), 0, 1 << 20, dtype=jnp.int32) % (spread + 1)
    counts = (MINB + extra).reshape(NB)
    chosen = jax.random.randint(third_key, (), 0, NB, dtype=jnp.int32)
    counts = jnp.where(jnp.arange(NB, dtype=jnp.int32) == chosen, MAXB, counts)
    return counts.astype(jnp.int32)


def steps_of(rng, dims, shards, low, top_value):
    factor_of, own = 1.0, jax.random.fold_in(rng, 6)
    for position, blocks in shards:
        heights = jnp.exp(jax.random.uniform(jax.random.fold_in(own, position), (blocks,), jnp.float32, low / len(shards), top_value / len(shards)))
        factor_of = factor_of * jnp.repeat(heights, dims[position] // blocks).reshape([-1 if axis == position else 1 for axis in range(len(dims))])
    return factor_of


def centred(own_key, shape, scale, most, cuts=(), kind=jnp.bfloat16):
    loudness = steps_of(own_key, shape, cuts, -0.22, 0.18) if cuts else 1.0
    result = jax.random.normal(own_key, shape, jnp.float32) * scale * loudness
    return jnp.minimum(jnp.maximum(result, -most), most).astype(kind)


def setup_inputs(seed: int = 0) -> dict:
    key_list = jax.random.split(jax.random.key(seed), 5)
    return {
        "matrix_blocks": centred(key_list[0], (NB, MAXB, BS, BS), (MAXB * BS // 2) ** -0.5, 0.078125, ((0, 128),)),
        "test_panel": centred(key_list[1], (NB * BS, K), 1.0, 6.0, ((0, 128),)),
        "column_blocks": draw_column_blocks(jax.random.fold_in(key_list[4], 71), 0),
        "row_counts": draw_row_counts(jax.random.fold_in(key_list[4], 71), 0),
    }


def reference(matrix_blocks, test_panel, column_blocks, row_counts):
    panel = test_panel.reshape(NB, BS, K)
    positions = jnp.arange(MAXB, dtype=jnp.int32)

    def one_row(pieces):
        blocks, columns, count = pieces
        picked = panel[columns.astype(jnp.int32)].astype(jnp.float32)
        picked = jnp.where((positions < count)[:, None, None], picked, jnp.float32(0.0))
        return jnp.einsum('bij,bjk->ik', blocks.astype(jnp.float32), picked, precision=lax.Precision.HIGHEST)
    sample = lax.map(one_row, (matrix_blocks, column_blocks, row_counts)).reshape(NB * BS, K)
    ortho, factor = jnp.linalg.qr(sample)
    signs = jnp.sign(jnp.diagonal(factor))
    scale = math.sqrt(NB * BS)
    return (ortho * signs[None, :] * scale, factor * signs[:, None] / scale)
```

```python
import functools

import jax
import jax.numpy as jnp
from jax import lax
from jax.experimental import pallas as pl
from jax.experimental.pallas import tpu as pltpu
from jax.sharding import PartitionSpec as P

MESH = pl.DeviceIdType.MESH
HI = lax.Precision.HIGHEST


PIECES = ((0, 176), (176, 176), (352, 160))
HALF = (96, 80, 80)
STEP = (0, 3, 1, 2)
N_COPIES = 156
GROUP = 6


def sample_kernel(cols_ref, counts_ref, blocks_ref, panel_ref, sample_ref, gram_ref, panels, held, table_v, table_s, local, twin_half, terms, send_sem, recv_sem, local_sem, line_send, line_recv, pair_send, pair_recv):
    me = lax.axis_index("row")
    core = me % 2
    coords = [me // 32, (me // 8) % 4, (me // 2) % 4]

    def device(at, which):
        return at[0] * 32 + at[1] * 8 + at[2] * 2 + which

    def shifted(axis, by):
        at = list(coords)
        at[axis] = (at[axis] + by) % 4
        return at

    sibling = device(coords, 1 - core)
    partners = [device(shifted(a, s), core) for a in range(3) for s in (1, 2, 3)] + [sibling]
    barrier = pltpu.get_barrier_semaphore()
    for other in partners:
        pl.semaphore_signal(barrier, inc=1, device_id=(other,), device_id_type=MESH)
    blocks_copy = pltpu.make_async_copy(blocks_ref, held, local_sem.at[0])
    blocks_copy.start()
    own = pltpu.make_async_copy(panel_ref, panels.at[coords[0], coords[1], coords[2], core], local_sem.at[1])
    own.start()
    pl.semaphore_wait(barrier, len(partners))

    started = []
    landed = {}

    def view(where, rows, which=core):
        return panels.at[where[0], where[1], where[2], which, pl.ds(rows[0], rows[1])]

    def push(key, src, dst, target):
        slot = len(started)
        copy = pltpu.make_async_remote_copy(
            src_ref=src, dst_ref=dst, send_sem=send_sem.at[slot], recv_sem=recv_sem.at[slot],
            device_id=(target,), device_id_type=MESH)
        copy.start()
        started.append(copy)
        landed[key] = copy

    def arrive(key):
        landed[key].wait_recv()

    def rows_of(p, part):
        first, count = PIECES[p]
        if part is None:
            return (first, count)
        cut = HALF[p]
        return (first, cut) if part == 0 else (first + cut, count - cut)

    def spot(p, ka, kb, kc):
        where = [None] * 3
        for axis, k in ((p, ka), ((p + 1) % 3, kb), ((p + 2) % 3, kc)):
            where[axis] = pl.ds(0, 4) if k is None else (coords[axis] + STEP[k]) % 4
        return where

    def send(key, p, axis, sign, where, rows, from_panel=False):
        src = panel_ref.at[pl.ds(rows[0], rows[1])] if from_panel else view(where, rows)
        push(key, src, view(where, rows), device(shifted(axis, sign), core))

    def twin(key, p, where, rows):
        push(key, view(where, rows), view(where, rows), sibling)

    PS = range(3)
    for p in PS:
        for k, sign in ((1, 1), (2, 3)):
            send((p, 1, k), p, p, sign, spot(p, 0, 0, 0), rows_of(p, None), True)
    for p in PS:
        for k, sign in ((1, 1), (2, 3)):
            send((p, 2, 0, k), p, (p + 1) % 3, sign, spot(p, 0, 0, 0), rows_of(p, None), True)

    lane = lax.broadcasted_iota(jnp.int32, (8, 128), 1)
    table = jnp.zeros((8, 128), jnp.int32)
    for r in range(2):
        def mark(s, found, r=r):
            column = cols_ref[r, s]
            holder = jnp.where(s < counts_ref[r], column >> 1, -1)
            return jnp.where(lane == holder, 1 + 2 * (r * 48 + s) + (column & 1), found)
        table = lax.fori_loop(0, 48, mark, table)
    table_v[...] = table
    table_copy = pltpu.make_async_copy(table_v, table_s, local_sem.at[2])
    table_copy.start()
    sample_ref[...] = jnp.zeros((512, 256), jnp.float32)

    for ka, sign, part in ((1, 1, 0), (2, 3, 1)):
        for p in PS:
            arrive((p, 1, ka))
            send((p, 1, 3, part), p, p, sign, spot(p, ka, 0, 0), rows_of(p, part))
            for k, s in ((1, 1), (2, 3)):
                send((p, 2, ka, k), p, (p + 1) % 3, s, spot(p, ka, 0, 0), rows_of(p, None))
    own.wait()
    table_copy.wait()

    def forward_b(ka):
        for kb, sign, part in ((1, 1, 0), (2, 3, 1)):
            for p in PS:
                arrive((p, 2, ka, kb))
                send((p, 2, ka, 3, part), p, (p + 1) % 3, sign, spot(p, ka, kb, 0), rows_of(p, part))

    def send_c(kb):
        for p in PS:
            for k, s in ((1, 1), (2, 3)):
                send((p, 3, kb, k), p, (p + 2) % 3, s, spot(p, None, kb, 0), rows_of(p, None))
        for p in PS:
            twin((p, 4, kb, 0), p, spot(p, None, kb, 0), rows_of(p, None))

    def forward_c(kb):
        for kc, sign, part in ((1, 1, 0), (2, 3, 1)):
            for p in PS:
                arrive((p, 3, kb, kc))
                send((p, 3, kb, 3, part), p, (p + 2) % 3, sign, spot(p, None, kb, kc), rows_of(p, part))
                twin((p, 4, kb, kc), p, spot(p, None, kb, kc), rows_of(p, None))

    def last_c(kb):
        for p in PS:
            arrive((p, 3, kb, 3, 0))
            arrive((p, 3, kb, 3, 1))
            twin((p, 4, kb, 3), p, spot(p, None, kb, 3), rows_of(p, None))

    def twins(pairs):
        for kb, kc in pairs:
            for p in PS:
                arrive((p, 4, kb, kc))

    def add_products(units):
        tops, bottoms, rights = [], [], []
        for shift, which in units:
            at = [(coords[i] + shift[i]) % 4 for i in range(3)]
            code = table_s[0, device(at, which)]
            index = jnp.maximum(code - 1, 0)
            slot = index >> 1
            block = held[jnp.where(slot >= 48, 1, 0), jnp.where(slot >= 48, slot - 48, slot)]
            none = jnp.zeros_like(block)
            tops.append(jnp.where((code > 0) & (slot < 48), block, none))
            bottoms.append(jnp.where((code > 0) & (slot >= 48), block, none))
            here = panels.at[at[0], at[1], at[2], which]
            rights.append(jnp.where((index & 1) == 0, here[:256], here[256:]))
        left = jnp.concatenate([jnp.concatenate(tops, axis=1), jnp.concatenate(bottoms, axis=1)], axis=0)
        sample_ref[...] += jnp.dot(left, jnp.concatenate(rights, axis=0), preferred_element_type=jnp.float32)

    def near(first, last):
        @pl.loop(first, last)
        def _(i):
            add_products([((i // 3 + 3, i % 3 + 3, k), w) for k in (3, 0, 1) for w in (0, 1)])

    def one_far(first, last):
        @pl.loop(first, last)
        def _(i):
            axis, u = i // 3, i % 3 + 3
            units = []
            for k in (3, 0, 1):
                shift = (jnp.where(axis == 0, 2, k), jnp.where(axis == 1, 2, jnp.where(axis == 0, k, u)), jnp.where(axis == 2, 2, u))
                units += [(shift, 0), (shift, 1)]
            add_products(units)

    def more_far():
        @pl.loop(0, 5)
        def _(i):
            units = []
            for j in (2 * i, 2 * i + 1):
                axis, u = j // 3, j % 3 + 3
                shift = tuple(jnp.where(axis == a, u, 2) for a in range(3))
                units += [(shift, 0), (shift, 1)]
            add_products(units)

    forward_b(0)
    for p in PS:
        arrive((p, 1, 3, 0))
        arrive((p, 1, 3, 1))
        for k, s in ((1, 1), (2, 3)):
            send((p, 2, 3, k), p, (p + 1) % 3, s, spot(p, 3, 0, 0), rows_of(p, None))
    send_c(0)
    forward_b(1)
    forward_b(2)
    forward_b(3)
    send_c(1)
    send_c(2)
    for p in PS:
        for ka in range(4):
            arrive((p, 2, ka, 3, 0))
            arrive((p, 2, ka, 3, 1))
    send_c(3)
    blocks_copy.wait()
    forward_c(0)
    forward_c(1)
    forward_c(2)
    twins([(kb, kc) for kb in range(3) for kc in range(3)])
    near(0, 6)
    forward_c(3)
    near(6, 9)
    last_c(0)
    last_c(1)
    last_c(2)
    twins([(3, kc) for kc in range(3)] + [(kb, 3) for kb in range(3)])
    one_far(0, 9)
    last_c(3)
    twins([(3, 3)])
    more_far()

    v = sample_ref[...]
    gram = lax.dot_general(v, v, (((0,), (0,)), ((), ())), precision=HI, preferred_element_type=jnp.float32)
    local[:128] = gram[:128, :128]
    local[128:256] = gram[:128, 128:]
    local[256:] = gram[128:, 128:]

    def half(which):
        return pl.ds(pl.multiple_of(which * 192, 64), 192)
    pair = pltpu.make_async_remote_copy(
        src_ref=local.at[half(1 - core)], dst_ref=twin_half, send_sem=pair_send.at[0], recv_sem=pair_recv.at[0],
        device_id=(sibling,), device_id_type=MESH)
    pair.start()
    pair.wait_recv()
    both = local[half(core)] + twin_half[...]
    parts = [both[64 * q:64 * q + 64] for q in PS]
    lines = []
    for t in range(3):
        here = []
        for q in PS:
            axis = (q + t) % 3
            mine = terms.at[t, q, coords[axis]]
            mine[...] = parts[q]
            for i in (2, 1, 3):
                copy = pltpu.make_async_remote_copy(
                    src_ref=mine, dst_ref=mine, send_sem=line_send.at[t, q, i - 1], recv_sem=line_recv.at[t, q, i - 1],
                    device_id=(device(shifted(axis, i), core),), device_id_type=MESH)
                copy.start()
                here.append(copy)
        for copy in here:
            copy.wait_recv()
        lines += here
        parts = [(terms[t, q, 0] + terms[t, q, 1]) + (terms[t, q, 2] + terms[t, q, 3]) for q in PS]
    for q in PS:
        gram_ref[pl.ds(pl.multiple_of(core * 192 + 64 * q, 64), 64)] = parts[q]
    back = pltpu.make_async_remote_copy(
        src_ref=gram_ref.at[half(core)], dst_ref=gram_ref.at[half(core)], send_sem=pair_send.at[1], recv_sem=pair_recv.at[1],
        device_id=(sibling,), device_id_type=MESH)
    back.start()
    back.wait_recv()
    for copy in started + lines + [pair, back]:
        copy.wait_send()
    assert len(started) == N_COPIES


def sample_and_gram(cols, counts, blocks, panel):
    return pl.pallas_call(
        sample_kernel,
        out_shape=(jax.ShapeDtypeStruct((512, 256), jnp.float32), jax.ShapeDtypeStruct((384, 128), jnp.float32)),
        in_specs=[pl.BlockSpec(memory_space=pltpu.SMEM)] * 2 + [pl.BlockSpec(memory_space=pl.ANY)] * 2,
        out_specs=(pl.BlockSpec(memory_space=pltpu.VMEM),) * 2,
        scratch_shapes=[
            pltpu.VMEM((4, 4, 4, 2, 512, 256), jnp.bfloat16),
            pltpu.VMEM((2, 48, 256, 256), jnp.bfloat16),
            pltpu.VMEM((8, 128), jnp.int32),
            pltpu.SMEM((8, 128), jnp.int32),
            pltpu.VMEM((384, 128), jnp.float32),
            pltpu.VMEM((192, 128), jnp.float32),
            pltpu.VMEM((3, 3, 4, 64, 128), jnp.float32),
            pltpu.SemaphoreType.DMA((N_COPIES,)),
            pltpu.SemaphoreType.DMA((N_COPIES,)),
            pltpu.SemaphoreType.DMA((3,)),
            pltpu.SemaphoreType.DMA((3, 3, 3)),
            pltpu.SemaphoreType.DMA((3, 3, 3)),
            pltpu.SemaphoreType.DMA((2,)),
            pltpu.SemaphoreType.DMA((2,)),
        ],
        compiler_params=pltpu.CompilerParams(collective_id=0, has_side_effects=True, vmem_limit_bytes=56 << 20),
        name="sample_gram",
    )(cols, counts, blocks, panel)


def dot(a, b, ca=1, cb=0):
    return lax.dot_general(a, b, (((ca,), (cb,)), ((), ())), precision=HI, preferred_element_type=jnp.float32)

def recip(x):
    r = pl.reciprocal(x, approx=True)
    return r * (2.0 - x * r)

def eliminate2(s, n=128):
    g = n // 8
    sub = lax.broadcasted_iota(jnp.int32, (8, n), 0)
    lane = lax.broadcasted_iota(jnp.int32, (8, n), 1)
    S = [s[8*i:8*i+8] for i in range(g)]
    W = [jnp.where(lane == sub + 8*i, 1.0, 0.0).astype(jnp.float32) for i in range(g)]
    for j in range(0, n, 2):
        k, r = divmod(j, 8)
        b0 = [None]*k + [jnp.broadcast_to(S[i][:, j:j+1], (8, n)) for i in range(k, g)]
        b1 = [None]*k + [jnp.broadcast_to(S[i][:, j+1:j+2], (8, n)) for i in range(k, g)]
        def row(x, q): return jnp.broadcast_to(x[q:q+1], (8, n))
        a = row(b0[k], r); b = row(b0[k], r+1); c = row(b1[k], r+1)
        s0 = row(S[k], r); s1 = row(S[k], r+1); w0 = row(W[k], r); w1 = row(W[k], r+1)
        idet = recip(a*c - b*b)
        t0 = (c*s0 - b*s1)*idet; t1 = (a*s1 - b*s0)*idet
        u0 = (c*w0 - b*w1)*idet; u1 = (a*w1 - b*w0)*idet
        ia = recip(a)
        l = b*ia
        for i in range(k, g):
            if i == k:
                m0 = jnp.where(sub > r+1, b0[i], 0.0); m1 = jnp.where(sub > r+1, b1[i], 0.0)
                ns = S[i] - m0*t0 - m1*t1
                nw = W[i] - m0*u0 - m1*u1
                S[i] = jnp.where(sub == r+1, ns - l*s0, ns)
                W[i] = jnp.where(sub == r+1, nw - l*w0, nw)
            else:
                S[i] = S[i] - b0[i]*t0 - b1[i]*t1
                W[i] = W[i] - b0[i]*u0 - b1[i]*u1
    return S, W

def finish(S, W, n=128):
    g = n // 8
    sub = lax.broadcasted_iota(jnp.int32, (8, n), 0)
    lane = lax.broadcasted_iota(jnp.int32, (8, n), 1)
    R, V = [], []
    for i in range(g):
        d = jnp.sum(jnp.where(lane == sub + 8*i, S[i], 0.0), axis=1, keepdims=True)
        q = lax.rsqrt(d)
        q = q*(1.5 - 0.5*d*q*q)
        R.append(jnp.where(lane >= sub + 8*i, S[i]*q, 0.0))
        V.append(W[i]*q)
    return jnp.concatenate(R, 0), jnp.concatenate(V, 0)

def factor(gram_ref, elim):
    R11, V11 = finish(*elim(gram_ref[:128]))
    R12 = dot(V11, gram_ref[128:256])
    s = gram_ref[256:] - dot(R12, R12, 0, 0)
    R22, V22 = finish(*elim(s))
    V21 = -dot(V22, dot(R12, V11, 0, 0))
    return R11, R12, R22, V11, V21, V22

def chol_kernel(elim, gram_ref, sample_ref, basis_ref, tri_ref):
    R11, R12, R22, V11, V21, V22 = factor(gram_ref, elim)
    sc = 1.0/256
    tri_ref[:128, :128] = R11*sc
    tri_ref[:128, 128:] = R12*sc
    tri_ref[128:, :128] = jnp.zeros((128, 128), jnp.float32)
    tri_ref[128:, 128:] = R22*sc
    s1 = sample_ref[:, :128]; s2 = sample_ref[:, 128:]
    basis_ref[:, :128] = dot(s1, V11*256.0, 1, 1)
    basis_ref[:, 128:] = dot(s1, V21*256.0, 1, 1) + dot(s2, V22*256.0, 1, 1)

def chol(gram, sample, elim=eliminate2):
    return pl.pallas_call(functools.partial(chol_kernel, elim),
        out_shape=(jax.ShapeDtypeStruct(sample.shape, jnp.float32), jax.ShapeDtypeStruct((256,256), jnp.float32)),
        in_specs=[pl.BlockSpec(memory_space=pltpu.VMEM)]*2, out_specs=(pl.BlockSpec(memory_space=pltpu.VMEM),)*2,
        compiler_params=pltpu.CompilerParams(vmem_limit_bytes=32<<20), name="chol")(gram, sample)


def per_device(matrix_blocks, test_panel, column_blocks, row_counts):
    values, gram = sample_and_gram(column_blocks, row_counts, matrix_blocks, test_panel)
    return chol(gram, values)


def solution(mesh):
    in_specs = (P("row", None, None, None), P("row", None), P("row", None), P("row"))
    return jax.shard_map(
        per_device, mesh=mesh, in_specs=in_specs, out_specs=(P("row", None), P()), check_vma=False
    )
```

```python
import functools

import jax
import jax.numpy as jnp
from jax import lax
from jax.experimental import pallas as pl
from jax.experimental.pallas import tpu as pltpu
from jax.sharding import PartitionSpec as P

MESH = pl.DeviceIdType.MESH
HI = lax.Precision.HIGHEST


PIECES = ((0, 176), (176, 176), (352, 160))
HALF = (96, 80, 80)
STEP = (0, 3, 1, 2)
N_COPIES = 180


def sample_kernel(cols_ref, counts_ref, blocks_ref, panel_ref, sample_out, gram_ref, panels, held, sample_ref, table_v, table_s, local, twin_half, terms, send_sem, recv_sem, local_sem, line_send, line_recv, pair_send, pair_recv):
    me = lax.axis_index("row")
    core = me % 2
    coords = [me // 32, (me // 8) % 4, (me // 2) % 4]

    def device(at, which):
        return at[0] * 32 + at[1] * 8 + at[2] * 2 + which

    def shifted(axis, by):
        at = list(coords)
        at[axis] = (at[axis] + by) % 4
        return at

    sibling = device(coords, 1 - core)
    partners = [device(shifted(a, s), core) for a in range(3) for s in (1, 2, 3)] + [sibling]
    barrier = pltpu.get_barrier_semaphore()
    for other in partners:
        pl.semaphore_signal(barrier, inc=1, device_id=(other,), device_id_type=MESH)
    blocks_copy = pltpu.make_async_copy(blocks_ref, held, local_sem.at[0])
    blocks_copy.start()
    own = pltpu.make_async_copy(panel_ref, panels.at[coords[0], coords[1], coords[2], core], local_sem.at[1])
    own.start()
    pl.semaphore_wait(barrier, len(partners))

    started = []
    landed = {}

    def view(where, rows, which=core):
        return panels.at[where[0], where[1], where[2], which, pl.ds(rows[0], rows[1])]

    def push(key, src, dst, target):
        slot = len(started)
        copy = pltpu.make_async_remote_copy(
            src_ref=src, dst_ref=dst, send_sem=send_sem.at[slot], recv_sem=recv_sem.at[slot],
            device_id=(target,), device_id_type=MESH)
        copy.start()
        started.append(copy)
        landed[key] = copy

    def arrive(key):
        landed[key].wait_recv()

    def rows_of(p, part, flip=0):
        first, count = PIECES[p]
        if part is None:
            return (first, count)
        cut = count - HALF[p] if flip else HALF[p]
        return (first, cut) if part == 0 else (first + cut, count - cut)

    def spot(p, ka, kb, kc, among=(0, 4)):
        where = [None] * 3
        for axis, k in ((p, ka), ((p + 1) % 3, kb), ((p + 2) % 3, kc)):
            where[axis] = pl.ds(*among) if k is None else (coords[axis] + STEP[k]) % 4
        return where

    def send(key, p, axis, sign, where, rows, from_panel=False):
        src = panel_ref.at[pl.ds(rows[0], rows[1])] if from_panel else view(where, rows)
        push(key, src, view(where, rows), device(shifted(axis, sign), core))

    def twin(key, p, where, rows):
        push(key, view(where, rows), view(where, rows), sibling)

    PS = range(3)
    for p in PS:
        for k, sign in ((1, 1), (2, 3)):
            send((p, 1, k), p, p, sign, spot(p, 0, 0, 0), rows_of(p, None), True)
    for p in PS:
        for k, sign in ((1, 1), (2, 3)):
            send((p, 2, 0, k), p, (p + 1) % 3, sign, spot(p, 0, 0, 0), rows_of(p, None), True)

    lane = lax.broadcasted_iota(jnp.int32, (8, 128), 1)
    table = jnp.zeros((8, 128), jnp.int32)
    for r in range(2):
        def mark(s, found, r=r):
            column = cols_ref[r, s]
            holder = jnp.where(s < counts_ref[r], column >> 1, -1)
            return jnp.where(lane == holder, 1 + 2 * (r * 48 + s) + (column & 1), found)
        table = lax.fori_loop(0, 48, mark, table)
    table_v[...] = table
    table_copy = pltpu.make_async_copy(table_v, table_s, local_sem.at[2])
    table_copy.start()
    sample_ref[...] = jnp.zeros((512, 256), jnp.float32)

    for ka, sign, part in ((1, 1, 0), (2, 3, 1)):
        for p in PS:
            arrive((p, 1, ka))
            send((p, 1, 3, part), p, p, sign, spot(p, ka, 0, 0), rows_of(p, part, p % 2))
            for k, s in ((1, 1), (2, 3)):
                send((p, 2, ka, k), p, (p + 1) % 3, s, spot(p, ka, 0, 0), rows_of(p, None))
    own.wait()
    table_copy.wait()

    def forward_b(ka):
        for kb, sign, part in ((1, 1, 0), (2, 3, 1)):
            for p in PS:
                arrive((p, 2, ka, kb))
                send((p, 2, ka, 3, part), p, (p + 1) % 3, sign, spot(p, ka, kb, 0), rows_of(p, part, ka % 2))

    def send_c(kb):
        for p in PS:
            for k, s in ((1, 1), (2, 3)):
                send((p, 3, kb, k), p, (p + 2) % 3, s, spot(p, None, kb, 0), rows_of(p, None))
        for p in PS:
            twin((p, 4, kb, 0), p, spot(p, None, kb, 0), rows_of(p, None))

    def cuts(kb):
        return ((0, 2), (2, 2)) if kb == 3 else ((0, 4),)

    def forward_c(kb):
        for kc, sign, part in ((1, 1, 0), (2, 3, 1)):
            for p in PS:
                arrive((p, 3, kb, kc))
                for among in cuts(kb):
                    send((p, 3, kb, 3, part, among), p, (p + 2) % 3, sign, spot(p, None, kb, kc, among), rows_of(p, part, kb % 2))
                twin((p, 4, kb, kc), p, spot(p, None, kb, kc), rows_of(p, None))

    def last_c(kb):
        for among in cuts(kb):
            for p in PS:
                for part in range(2):
                    arrive((p, 3, kb, 3, part, among))
                    twin((p, 4, kb, 3, part, among), p, spot(p, None, kb, 3, among), rows_of(p, part, kb % 2))

    def twins(pairs):
        for kb, kc in pairs:
            for p in PS:
                if kc < 3:
                    arrive((p, 4, kb, kc))
                    continue
                for among in cuts(kb):
                    for part in range(2):
                        arrive((p, 4, kb, 3, part, among))

    def add_products(units):
        tops, bottoms, rights = [], [], []
        for shift, which in units:
            at = [(coords[i] + shift[i]) % 4 for i in range(3)]
            code = table_s[0, device(at, which)]
            index = jnp.maximum(code - 1, 0)
            slot = index >> 1
            block = held[jnp.where(slot >= 48, 1, 0), jnp.where(slot >= 48, slot - 48, slot)]
            none = jnp.zeros_like(block)
            tops.append(jnp.where((code > 0) & (slot < 48), block, none))
            bottoms.append(jnp.where((code > 0) & (slot >= 48), block, none))
            here = panels.at[at[0], at[1], at[2], which]
            rights.append(jnp.where((index & 1) == 0, here[:256], here[256:]))
        left = jnp.concatenate([jnp.concatenate(tops, axis=1), jnp.concatenate(bottoms, axis=1)], axis=0)
        sample_ref[...] += jnp.dot(left, jnp.concatenate(rights, axis=0), preferred_element_type=jnp.float32)

    def near(first, last):
        @pl.loop(first, last)
        def _(i):
            add_products([((i // 3 + 3, i % 3 + 3, k), w) for k in (3, 0, 1) for w in (0, 1)])

    def one_far(kb, which):
        @pl.loop(0, 3)
        def _(i):
            add_products([
                (tuple(jnp.where(axis == i, 2, jnp.where(axis == (i + 2) % 3, STEP[kb], k)) for axis in range(3)), which)
                for k in (3, 0, 1)])

    def more_far(which):
        @pl.loop(0, 2)
        def _(i):
            units = []
            for n in range(5):
                j = 5 * i + n
                axis, u = j // 3, j % 3 + 3
                units.append((tuple(jnp.where(axis == a, u, 2) for a in range(3)), which))
            add_products(units)

    forward_b(0)
    for p in PS:
        arrive((p, 1, 3, 0))
        arrive((p, 1, 3, 1))
        for k, s in ((1, 1), (2, 3)):
            send((p, 2, 3, k), p, (p + 1) % 3, s, spot(p, 3, 0, 0), rows_of(p, None))
    send_c(0)
    forward_b(1)
    forward_b(2)
    forward_b(3)
    send_c(1)
    send_c(2)
    for p in PS:
        for ka in range(4):
            arrive((p, 2, ka, 3, 0))
            arrive((p, 2, ka, 3, 1))
    send_c(3)
    blocks_copy.wait()
    forward_c(0)
    forward_c(1)
    forward_c(2)
    twins([(kb, kc) for kb in range(3) for kc in range(3)])
    near(0, 6)
    forward_c(3)
    near(6, 9)
    last_c(0)
    one_far(0, core)
    last_c(1)
    twins([(3, kc) for kc in range(3)] + [(0, 3)])
    one_far(0, 1 - core)
    one_far(1, core)
    last_c(2)
    twins([(1, 3)])
    one_far(1, 1 - core)
    one_far(2, core)
    last_c(3)
    twins([(2, 3)])
    one_far(2, 1 - core)
    more_far(core)
    twins([(3, 3)])
    more_far(1 - core)

    sample_copy = pltpu.make_async_copy(sample_ref, sample_out, local_sem.at[3])
    sample_copy.start()
    v = sample_ref[...]
    gram = lax.dot_general(v, v, (((0,), (0,)), ((), ())), precision=HI, preferred_element_type=jnp.float32)
    local[:128] = gram[:128, :128]
    local[128:256] = gram[:128, 128:]
    local[256:] = gram[128:, 128:]

    def part_rows(which, q):
        return pl.ds(pl.multiple_of(which * 192 + 64 * q, 64), 64)

    pairs, lines, backs = [], {}, []
    for q in PS:
        pairs.append(pltpu.make_async_remote_copy(
            src_ref=local.at[part_rows(1 - core, q)], dst_ref=twin_half.at[q], send_sem=pair_send.at[0, q], recv_sem=pair_recv.at[0, q],
            device_id=(sibling,), device_id_type=MESH))
        pairs[q].start()

    def along(t, q, value):
        axis = (q + t) % 3
        mine = terms.at[t, q, coords[axis]]
        mine[...] = value
        for i in (2, 1, 3):
            copy = pltpu.make_async_remote_copy(
                src_ref=mine, dst_ref=mine, send_sem=line_send.at[t, q, i - 1], recv_sem=line_recv.at[t, q, i - 1],
                device_id=(device(shifted(axis, i), core),), device_id_type=MESH)
            copy.start()
            lines[t, q, i] = copy

    for q in PS:
        pairs[q].wait_recv()
        along(0, q, local[part_rows(core, q)] + twin_half[q])
    for t in range(3):
        for q in PS:
            for i in (1, 3, 2):
                lines[t, q, i].wait_recv()
            total = (terms[t, q, 0] + terms[t, q, 1]) + (terms[t, q, 2] + terms[t, q, 3])
            if t < 2:
                along(t + 1, q, total)
                continue
            gram_ref[part_rows(core, q)] = total
            backs.append(pltpu.make_async_remote_copy(
                src_ref=gram_ref.at[part_rows(core, q)], dst_ref=gram_ref.at[part_rows(core, q)], send_sem=pair_send.at[1, q], recv_sem=pair_recv.at[1, q],
                device_id=(sibling,), device_id_type=MESH))
            backs[q].start()
    for copy in backs:
        copy.wait_recv()
    for copy in started + list(lines.values()) + pairs + backs:
        copy.wait_send()
    sample_copy.wait()
    assert len(started) == N_COPIES, len(started)


def sample_and_gram(cols, counts, blocks, panel):
    return pl.pallas_call(
        sample_kernel,
        out_shape=(jax.ShapeDtypeStruct((512, 256), jnp.float32), jax.ShapeDtypeStruct((384, 128), jnp.float32)),
        in_specs=[pl.BlockSpec(memory_space=pltpu.SMEM)] * 2 + [pl.BlockSpec(memory_space=pl.ANY)] * 2,
        out_specs=(pl.BlockSpec(memory_space=pl.ANY), pl.BlockSpec(memory_space=pltpu.VMEM)),
        scratch_shapes=[
            pltpu.VMEM((4, 4, 4, 2, 512, 256), jnp.bfloat16),
            pltpu.VMEM((2, 48, 256, 256), jnp.bfloat16),
            pltpu.VMEM((512, 256), jnp.float32),
            pltpu.VMEM((8, 128), jnp.int32),
            pltpu.SMEM((8, 128), jnp.int32),
            pltpu.VMEM((384, 128), jnp.float32),
            pltpu.VMEM((3, 64, 128), jnp.float32),
            pltpu.VMEM((3, 3, 4, 64, 128), jnp.float32),
            pltpu.SemaphoreType.DMA((N_COPIES,)),
            pltpu.SemaphoreType.DMA((N_COPIES,)),
            pltpu.SemaphoreType.DMA((4,)),
            pltpu.SemaphoreType.DMA((3, 3, 3)),
            pltpu.SemaphoreType.DMA((3, 3, 3)),
            pltpu.SemaphoreType.DMA((2, 3)),
            pltpu.SemaphoreType.DMA((2, 3)),
        ],
        compiler_params=pltpu.CompilerParams(collective_id=0, has_side_effects=True, vmem_limit_bytes=56 << 20),
        name="sample_gram",
    )(cols, counts, blocks, panel)


def dot(a, b, ca=1, cb=0):
    return lax.dot_general(a, b, (((ca,), (cb,)), ((), ())), precision=HI, preferred_element_type=jnp.float32)


def reciprocal(x):
    r = pl.reciprocal(x, approx=True)
    return r * (2.0 - x * r)


def factor_half(s, n=128):
    tiles = n // 8
    sub = lax.broadcasted_iota(jnp.int32, (8, n), 0)
    lane = lax.broadcasted_iota(jnp.int32, (8, n), 1)
    S = [s[8 * i:8 * i + 8] for i in range(tiles)]
    W = [jnp.where(lane == sub + 8 * i, 1.0, 0.0).astype(jnp.float32) for i in range(tiles)]

    def row(x, i):
        return jnp.broadcast_to(x[i:i + 1], (8, n))

    def column(x, j):
        return jnp.broadcast_to(x[:, j:j + 1], (8, n))

    for k in range(tiles):
        cols = [column(S[k], 8 * k + j) for j in range(8)]
        e = {(i, j): row(cols[j], i) for j in range(8) for i in range(j + 1)}
        r = [row(S[k], i) for i in range(8)]
        w = [row(W[k], i) for i in range(8)]
        inv, g, ahead = {}, {}, {}
        follow = k + 1 < tiles
        side = [column(S[k + 1], 8 * k + q) for q in range(8)] if follow else None
        kept = list(side) if follow else None
        for j in range(0, 8, 2):
            a, b, c = e[j, j], e[j, j + 1], e[j + 1, j + 1]
            det = a * c - b * b
            rough = pl.reciprocal(det, approx=True)
            near = 2.0 - det * rough
            inv[j] = rough * near
            ahead[j] = c * r[j] - b * r[j + 1], a * r[j + 1] - b * r[j], c * w[j] - b * w[j + 1], a * w[j + 1] - b * w[j]
            if follow:
                S[k + 1] = S[k + 1] - ((side[j] * ahead[j][0] + side[j + 1] * ahead[j][1]) * rough) * near
            for i in range(j + 2, 8):
                x, y = e[j, i], e[j + 1, i]
                n0, n1 = c * x - b * y, a * y - b * x
                for q in range(i, 8):
                    e[i, q] = e[i, q] - ((n0 * e[j, q] + n1 * e[j + 1, q]) * rough) * near
                g[i, j], g[i, j + 1] = n0 * inv[j], n1 * inv[j]
                if follow:
                    side[i] = side[i] - (g[i, j] * side[j] + g[i, j + 1] * side[j + 1])
                r[i] = r[i] - (g[i, j] * r[j] + g[i, j + 1] * r[j + 1])
                w[i] = w[i] - (g[i, j] * w[j] + g[i, j + 1] * w[j + 1])
        if k + 1 < tiles:
            t, u = [None] * 8, [None] * 8
            for j in (6, 4, 2, 0):
                t[j], t[j + 1], u[j], u[j + 1] = [v * inv[j] for v in ahead[j]]
                for m in range(j + 2, 8, 2):
                    for h in (j, j + 1):
                        t[h] = t[h] - (g[m, h] * t[m] + g[m + 1, h] * t[m + 1])
                        u[h] = u[h] - (g[m, h] * u[m] + g[m + 1, h] * u[m + 1])
            for i in range(k + 1, tiles):
                c = kept if i == k + 1 else [column(S[i], 8 * k + q) for q in range(8)]
                S[i] = S[i] if i == k + 1 else ((S[i] - (c[6] * t[6] + c[7] * t[7])) - (c[4] * t[4] + c[5] * t[5])) - (c[2] * t[2] + c[3] * t[3]) - (c[0] * t[0] + c[1] * t[1])
                W[i] = ((W[i] - (c[6] * u[6] + c[7] * u[7])) - (c[4] * u[4] + c[5] * u[5])) - (c[2] * u[2] + c[3] * u[3]) - (c[0] * u[0] + c[1] * u[1])
        for j in range(0, 8, 2):
            slope = e[j, j + 1] * reciprocal(e[j, j])
            r[j + 1] = r[j + 1] - slope * r[j]
            w[j + 1] = w[j + 1] - slope * w[j]
            e[j + 1, j + 1] = e[j + 1, j + 1] - slope * e[j, j + 1]
        new_s, new_w = r[0], w[0]
        d = e[0, 0]
        for i in range(1, 8):
            new_s = jnp.where(sub == i, r[i], new_s)
            new_w = jnp.where(sub == i, w[i], new_w)
            d = jnp.where(sub == i, e[i, i], d)
        q = lax.rsqrt(d)
        q = q * (1.5 - 0.5 * d * q * q)
        S[k] = jnp.where(lane >= sub + 8 * k, new_s * q, 0.0)
        W[k] = new_w * q
    return jnp.concatenate(S, axis=0), jnp.concatenate(W, axis=0)


def chol_kernel(gram_hbm, sample_hbm, basis_ref, tri_ref, gram_ref, sample_ref, sems):
    gram_copy = pltpu.make_async_copy(gram_hbm, gram_ref, sems.at[0])
    sample_copy = pltpu.make_async_copy(sample_hbm, sample_ref, sems.at[1])
    gram_copy.start()
    sample_copy.start()
    gram_copy.wait()
    R11, V11 = factor_half(gram_ref[:128])
    R12 = dot(V11, gram_ref[128:256])
    rest = gram_ref[256:] - dot(R12, R12, 0, 0)
    scale = 1.0 / 256
    sample_copy.wait()
    first = dot(sample_ref[:, :128], V11 * 256.0, 1, 1)
    second = sample_ref[:, 128:] * 256.0 - dot(first, R12)
    basis_ref[:, :128] = first
    tri_ref[:128, :128] = R11 * scale
    tri_ref[:128, 128:] = R12 * scale
    tri_ref[128:, :128] = jnp.zeros((128, 128), jnp.float32)
    R22, V22 = factor_half(rest)
    tri_ref[128:, 128:] = R22 * scale
    basis_ref[:, 128:] = dot(second, V22, 1, 1)


def chol(gram, values):
    return pl.pallas_call(
        chol_kernel,
        out_shape=(jax.ShapeDtypeStruct((512, 256), jnp.float32), jax.ShapeDtypeStruct((256, 256), jnp.float32)),
        in_specs=[pl.BlockSpec(memory_space=pl.ANY)] * 2,
        out_specs=(pl.BlockSpec(memory_space=pltpu.VMEM),) * 2,
        scratch_shapes=[pltpu.VMEM((384, 128), jnp.float32), pltpu.VMEM((512, 256), jnp.float32), pltpu.SemaphoreType.DMA((2,))],
        compiler_params=pltpu.CompilerParams(vmem_limit_bytes=56 << 20),
        name="factor_basis",
    )(gram, values)


def per_device(matrix_blocks, test_panel, column_blocks, row_counts):
    values, gram = sample_and_gram(column_blocks, row_counts, matrix_blocks, test_panel)
    return chol(gram, values)


def solution(mesh):
    in_specs = (P("row", None, None, None), P("row", None), P("row", None), P("row"))
    return jax.shard_map(
        per_device, mesh=mesh, in_specs=in_specs, out_specs=(P("row", None), P()), check_vma=False
    )
```

```python
import functools

import jax
import jax.numpy as jnp
from jax import lax
from jax.experimental import pallas as pl
from jax.experimental.pallas import tpu as pltpu
from jax.sharding import PartitionSpec as P

MESH = pl.DeviceIdType.MESH
HI = lax.Precision.HIGHEST


PIECES = ((0, 160), (160, 176), (336, 176))
HALF = (80, 96, 80)
STEP = (0, 3, 1, 2)
N_COPIES = 180


def sample_kernel(cols_ref, counts_ref, blocks_ref, panel_ref, sample_out, gram_ref, panels, held, sample_ref, table_v, table_s, local, twin_half, terms, send_sem, recv_sem, local_sem, line_send, line_recv, pair_send, pair_recv):
    me = lax.axis_index("row")
    core = me % 2
    coords = [me // 32, (me // 8) % 4, (me // 2) % 4]

    def device(at, which):
        return at[0] * 32 + at[1] * 8 + at[2] * 2 + which

    def shifted(axis, by):
        at = list(coords)
        at[axis] = (at[axis] + by) % 4
        return at

    sibling = device(coords, 1 - core)
    partners = [device(shifted(a, s), core) for a in range(3) for s in (1, 2, 3)] + [sibling]
    barrier = pltpu.get_barrier_semaphore()
    for other in partners:
        pl.semaphore_signal(barrier, inc=1, device_id=(other,), device_id_type=MESH)
    blocks_copy = pltpu.make_async_copy(blocks_ref, held, local_sem.at[0])
    blocks_copy.start()
    own = pltpu.make_async_copy(panel_ref, panels.at[coords[0], coords[1], coords[2], core], local_sem.at[1])
    own.start()
    pl.semaphore_wait(barrier, len(partners))

    started = []
    landed = {}

    def view(where, rows, which=core):
        return panels.at[where[0], where[1], where[2], which, pl.ds(rows[0], rows[1])]

    def push(key, src, dst, target):
        slot = len(started)
        copy = pltpu.make_async_remote_copy(
            src_ref=src, dst_ref=dst, send_sem=send_sem.at[slot], recv_sem=recv_sem.at[slot],
            device_id=(target,), device_id_type=MESH)
        copy.start()
        started.append(copy)
        landed[key] = copy

    def arrive(key):
        landed[key].wait_recv()

    def rows_of(p, part, flip=0):
        first, count = PIECES[p]
        if part is None:
            return (first, count)
        cut = count - HALF[p] if flip else HALF[p]
        return (first, cut) if part == 0 else (first + cut, count - cut)

    def spot(p, ka, kb, kc, among=(0, 4)):
        where = [None] * 3
        for axis, k in ((p, ka), ((p + 1) % 3, kb), ((p + 2) % 3, kc)):
            where[axis] = pl.ds(*among) if k is None else (coords[axis] + STEP[k]) % 4
        return where

    def send(key, p, axis, sign, where, rows, from_panel=False):
        src = panel_ref.at[pl.ds(rows[0], rows[1])] if from_panel else view(where, rows)
        push(key, src, view(where, rows), device(shifted(axis, sign), core))

    def twin(key, p, where, rows):
        push(key, view(where, rows), view(where, rows), sibling)

    PS = range(3)
    for p in PS:
        for k, sign in ((1, 1), (2, 3)):
            send((p, 1, k), p, p, sign, spot(p, 0, 0, 0), rows_of(p, None), True)
    for p in PS:
        for k, sign in ((1, 1), (2, 3)):
            send((p, 2, 0, k), p, (p + 1) % 3, sign, spot(p, 0, 0, 0), rows_of(p, None), True)

    lane = lax.broadcasted_iota(jnp.int32, (8, 128), 1)
    table = jnp.zeros((8, 128), jnp.int32)
    for r in range(2):
        def mark(s, found, r=r):
            column = cols_ref[r, s]
            holder = jnp.where(s < counts_ref[r], column >> 1, -1)
            return jnp.where(lane == holder, 1 + 2 * (r * 48 + s) + (column & 1), found)
        table = lax.fori_loop(0, 48, mark, table)
    table_v[...] = table
    table_copy = pltpu.make_async_copy(table_v, table_s, local_sem.at[2])
    table_copy.start()
    sample_ref[...] = jnp.zeros((512, 256), jnp.float32)

    for ka, sign, part in ((1, 1, 0), (2, 3, 1)):
        for p in PS:
            arrive((p, 1, ka))
            send((p, 1, 3, part), p, p, sign, spot(p, ka, 0, 0), rows_of(p, part, p % 2))
            for k, s in ((1, 1), (2, 3)):
                send((p, 2, ka, k), p, (p + 1) % 3, s, spot(p, ka, 0, 0), rows_of(p, None))
    own.wait()
    table_copy.wait()

    def forward_b(ka):
        for kb, sign, part in ((1, 1, 0), (2, 3, 1)):
            for p in PS:
                arrive((p, 2, ka, kb))
                send((p, 2, ka, 3, part), p, (p + 1) % 3, sign, spot(p, ka, kb, 0), rows_of(p, part, ka % 2))

    def send_c(kb):
        for p in PS:
            for k, s in ((1, 1), (2, 3)):
                send((p, 3, kb, k), p, (p + 2) % 3, s, spot(p, None, kb, 0), rows_of(p, None))
        for p in PS:
            twin((p, 4, kb, 0), p, spot(p, None, kb, 0), rows_of(p, None))

    def cuts(kb):
        return ((0, 2), (2, 2)) if kb == 3 else ((0, 4),)

    def forward_c(kb):
        for kc, sign, part in ((1, 1, 0), (2, 3, 1)):
            for p in PS:
                arrive((p, 3, kb, kc))
                for among in cuts(kb):
                    send((p, 3, kb, 3, part, among), p, (p + 2) % 3, sign, spot(p, None, kb, kc, among), rows_of(p, part, kb % 2))
                twin((p, 4, kb, kc), p, spot(p, None, kb, kc), rows_of(p, None))

    def last_c(kb):
        for among in cuts(kb):
            for p in PS:
                for part in range(2):
                    arrive((p, 3, kb, 3, part, among))
                    twin((p, 4, kb, 3, part, among), p, spot(p, None, kb, 3, among), rows_of(p, part, kb % 2))

    def twins(pairs):
        for kb, kc in pairs:
            for p in PS:
                if kc < 3:
                    arrive((p, 4, kb, kc))
                    continue
                for among in cuts(kb):
                    for part in range(2):
                        arrive((p, 4, kb, 3, part, among))

    def add_products(units):
        tops, bottoms, rights = [], [], []
        for shift, which in units:
            at = [(coords[i] + shift[i]) % 4 for i in range(3)]
            code = table_s[0, device(at, which)]
            index = jnp.maximum(code - 1, 0)
            slot = index >> 1
            block = held[jnp.where(slot >= 48, 1, 0), jnp.where(slot >= 48, slot - 48, slot)]
            none = jnp.zeros_like(block)
            tops.append(jnp.where((code > 0) & (slot < 48), block, none))
            bottoms.append(jnp.where((code > 0) & (slot >= 48), block, none))
            here = panels.at[at[0], at[1], at[2], which]
            rights.append(jnp.where((index & 1) == 0, here[:256], here[256:]))
        left = jnp.concatenate([jnp.concatenate(tops, axis=1), jnp.concatenate(bottoms, axis=1)], axis=0)
        sample_ref[...] += jnp.dot(left, jnp.concatenate(rights, axis=0), preferred_element_type=jnp.float32)

    def near(first, last):
        @pl.loop(first, last)
        def _(i):
            add_products([((i // 3 + 3, i % 3 + 3, k), w) for k in (3, 0, 1) for w in (0, 1)])

    def one_far(kb, which):
        @pl.loop(0, 3)
        def _(i):
            add_products([
                (tuple(jnp.where(axis == i, 2, jnp.where(axis == (i + 2) % 3, STEP[kb], k)) for axis in range(3)), which)
                for k in (3, 0, 1)])

    def more_far(which):
        @pl.loop(0, 2)
        def _(i):
            units = []
            for n in range(5):
                j = 5 * i + n
                axis, u = j // 3, j % 3 + 3
                units.append((tuple(jnp.where(axis == a, u, 2) for a in range(3)), which))
            add_products(units)

    forward_b(0)
    for p in PS:
        arrive((p, 1, 3, 0))
        arrive((p, 1, 3, 1))
        for k, s in ((1, 1), (2, 3)):
            send((p, 2, 3, k), p, (p + 1) % 3, s, spot(p, 3, 0, 0), rows_of(p, None))
    send_c(0)
    forward_b(1)
    forward_b(2)
    forward_b(3)
    send_c(1)
    send_c(2)
    for p in PS:
        for ka in range(4):
            arrive((p, 2, ka, 3, 0))
            arrive((p, 2, ka, 3, 1))
    send_c(3)
    blocks_copy.wait()
    forward_c(0)
    forward_c(1)
    forward_c(2)
    twins([(kb, kc) for kb in range(3) for kc in range(3)])
    near(0, 6)
    forward_c(3)
    near(6, 9)
    last_c(0)
    one_far(0, core)
    last_c(1)
    twins([(3, kc) for kc in range(3)] + [(0, 3)])
    one_far(0, 1 - core)
    one_far(1, core)
    last_c(2)
    twins([(1, 3)])
    one_far(1, 1 - core)
    one_far(2, core)
    last_c(3)
    twins([(2, 3)])
    one_far(2, 1 - core)
    more_far(core)
    twins([(3, 3)])
    more_far(1 - core)

    sample_copy = pltpu.make_async_copy(sample_ref, sample_out, local_sem.at[3])
    sample_copy.start()
    v = sample_ref[...]
    gram = lax.dot_general(v, v, (((0,), (0,)), ((), ())), precision=HI, preferred_element_type=jnp.float32)
    local[:128] = gram[:128, :128]
    local[128:256] = gram[:128, 128:]
    local[256:] = gram[128:, 128:]

    def part_rows(which, q):
        return pl.ds(pl.multiple_of(which * 192 + 64 * q, 64), 64)

    pairs, lines, backs = [], {}, []
    for q in PS:
        pairs.append(pltpu.make_async_remote_copy(
            src_ref=local.at[part_rows(1 - core, q)], dst_ref=twin_half.at[q], send_sem=pair_send.at[0, q], recv_sem=pair_recv.at[0, q],
            device_id=(sibling,), device_id_type=MESH))
        pairs[q].start()

    def along(t, q, value):
        axis = (q + t) % 3
        mine = terms.at[t, q, coords[axis]]
        mine[...] = value
        for i in (2, 1, 3):
            copy = pltpu.make_async_remote_copy(
                src_ref=mine, dst_ref=mine, send_sem=line_send.at[t, q, i - 1], recv_sem=line_recv.at[t, q, i - 1],
                device_id=(device(shifted(axis, i), core),), device_id_type=MESH)
            copy.start()
            lines[t, q, i] = copy

    for q in PS:
        pairs[q].wait_recv()
        along(0, q, local[part_rows(core, q)] + twin_half[q])
    for t in range(3):
        for q in PS:
            for i in (1, 3, 2):
                lines[t, q, i].wait_recv()
            total = (terms[t, q, 0] + terms[t, q, 1]) + (terms[t, q, 2] + terms[t, q, 3])
            if t < 2:
                along(t + 1, q, total)
                continue
            gram_ref[part_rows(core, q)] = total
            backs.append(pltpu.make_async_remote_copy(
                src_ref=gram_ref.at[part_rows(core, q)], dst_ref=gram_ref.at[part_rows(core, q)], send_sem=pair_send.at[1, q], recv_sem=pair_recv.at[1, q],
                device_id=(sibling,), device_id_type=MESH))
            backs[q].start()
    for copy in backs:
        copy.wait_recv()
    for copy in started + list(lines.values()) + pairs + backs:
        copy.wait_send()
    sample_copy.wait()
    assert len(started) == N_COPIES, len(started)


def sample_and_gram(cols, counts, blocks, panel):
    return pl.pallas_call(
        sample_kernel,
        out_shape=(jax.ShapeDtypeStruct((512, 256), jnp.float32), jax.ShapeDtypeStruct((384, 128), jnp.float32)),
        in_specs=[pl.BlockSpec(memory_space=pltpu.SMEM)] * 2 + [pl.BlockSpec(memory_space=pl.ANY)] * 2,
        out_specs=(pl.BlockSpec(memory_space=pl.ANY), pl.BlockSpec(memory_space=pltpu.VMEM)),
        scratch_shapes=[
            pltpu.VMEM((4, 4, 4, 2, 512, 256), jnp.bfloat16),
            pltpu.VMEM((2, 48, 256, 256), jnp.bfloat16),
            pltpu.VMEM((512, 256), jnp.float32),
            pltpu.VMEM((8, 128), jnp.int32),
            pltpu.SMEM((8, 128), jnp.int32),
            pltpu.VMEM((384, 128), jnp.float32),
            pltpu.VMEM((3, 64, 128), jnp.float32),
            pltpu.VMEM((3, 3, 4, 64, 128), jnp.float32),
            pltpu.SemaphoreType.DMA((N_COPIES,)),
            pltpu.SemaphoreType.DMA((N_COPIES,)),
            pltpu.SemaphoreType.DMA((4,)),
            pltpu.SemaphoreType.DMA((3, 3, 3)),
            pltpu.SemaphoreType.DMA((3, 3, 3)),
            pltpu.SemaphoreType.DMA((2, 3)),
            pltpu.SemaphoreType.DMA((2, 3)),
        ],
        compiler_params=pltpu.CompilerParams(collective_id=0, has_side_effects=True, vmem_limit_bytes=56 << 20),
        name="sample_gram",
    )(cols, counts, blocks, panel)


def dot(a, b, ca=1, cb=0):
    return lax.dot_general(a, b, (((ca,), (cb,)), ((), ())), precision=HI, preferred_element_type=jnp.float32)


def factor_half(s, spread, n=128):
    tiles = n // 8
    sub = lax.broadcasted_iota(jnp.int32, (8, n), 0)
    lane = lax.broadcasted_iota(jnp.int32, (8, n), 1)
    S = [s[8 * i:8 * i + 8] for i in range(tiles)]
    W = [jnp.where(lane == sub + 8 * i, 1.0, 0.0).astype(jnp.float32) for i in range(tiles)]

    def row(place, i):
        return spread[pl.ds(8 * place + i, 8, stride=0), :]

    def put(place, x):
        spread[8 * place:8 * place + 8, :] = x

    def column(x, j):
        return jnp.broadcast_to(x[:, j:j + 1], (8, n))

    for k in range(tiles):
        cols = [column(S[k], 8 * k + j) for j in range(8)]
        for j in range(8):
            put(10 * k + j, cols[j])
        put(10 * k + 8, S[k])
        put(10 * k + 9, W[k])
        e = {(i, j): row(10 * k + j, i) for j in range(8) for i in range(j + 1)}
        r = [row(10 * k + 8, i) for i in range(8)]
        w = [row(10 * k + 9, i) for i in range(8)]
        inv, g, ahead = {}, {}, {}
        follow = k + 1 < tiles
        side = [column(S[k + 1], 8 * k + q) for q in range(8)] if follow else None
        kept = list(side) if follow else None
        for j in range(0, 8, 2):
            a, b, c = e[j, j], e[j, j + 1], e[j + 1, j + 1]
            det = a * c - b * b
            inv[j] = pl.reciprocal(det, approx=True)
            ahead[j] = c * r[j] - b * r[j + 1], a * r[j + 1] - b * r[j], c * w[j] - b * w[j + 1], a * w[j + 1] - b * w[j]
            if follow:
                S[k + 1] = S[k + 1] - ((side[j] * ahead[j][0] + side[j + 1] * ahead[j][1]) * inv[j])
            for i in range(j + 2, 8):
                x, y = e[j, i], e[j + 1, i]
                n0, n1 = c * x - b * y, a * y - b * x
                for q in range(i, 8):
                    e[i, q] = e[i, q] - ((n0 * e[j, q] + n1 * e[j + 1, q]) * inv[j])
                g[i, j], g[i, j + 1] = n0 * inv[j], n1 * inv[j]
                if follow:
                    side[i] = side[i] - (g[i, j] * side[j] + g[i, j + 1] * side[j + 1])
                r[i] = r[i] - (g[i, j] * r[j] + g[i, j + 1] * r[j + 1])
                w[i] = w[i] - (g[i, j] * w[j] + g[i, j + 1] * w[j + 1])
        if k + 1 < tiles:
            t, u = [None] * 8, [None] * 8
            for j in (6, 4, 2, 0):
                t[j], t[j + 1], u[j], u[j + 1] = [v * inv[j] for v in ahead[j]]
                for m in range(j + 2, 8, 2):
                    for h in (j, j + 1):
                        t[h] = t[h] - (g[m, h] * t[m] + g[m + 1, h] * t[m + 1])
                        u[h] = u[h] - (g[m, h] * u[m] + g[m + 1, h] * u[m + 1])
            for i in range(k + 1, tiles):
                c = kept if i == k + 1 else [column(S[i], 8 * k + q) for q in range(8)]
                S[i] = S[i] if i == k + 1 else ((S[i] - (c[6] * t[6] + c[7] * t[7])) - (c[4] * t[4] + c[5] * t[5])) - (c[2] * t[2] + c[3] * t[3]) - (c[0] * t[0] + c[1] * t[1])
                W[i] = ((W[i] - (c[6] * u[6] + c[7] * u[7])) - (c[4] * u[4] + c[5] * u[5])) - (c[2] * u[2] + c[3] * u[3]) - (c[0] * u[0] + c[1] * u[1])
        for j in range(0, 8, 2):
            slope = e[j, j + 1] * pl.reciprocal(e[j, j], approx=True)
            r[j + 1] = r[j + 1] - slope * r[j]
            w[j + 1] = w[j + 1] - slope * w[j]
            e[j + 1, j + 1] = e[j + 1, j + 1] - slope * e[j, j + 1]
        new_s, new_w = r[0], w[0]
        d = e[0, 0]
        for i in range(1, 8):
            new_s = jnp.where(sub == i, r[i], new_s)
            new_w = jnp.where(sub == i, w[i], new_w)
            d = jnp.where(sub == i, e[i, i], d)
        q = lax.rsqrt(d)
        S[k] = jnp.where(lane >= sub + 8 * k, new_s * q, 0.0)
        W[k] = new_w * q
    return jnp.concatenate(S, axis=0), jnp.concatenate(W, axis=0)


def chol_kernel(gram_hbm, sample_hbm, basis_ref, tri_ref, gram_ref, sample_ref, spread, sems):
    gram_copy = pltpu.make_async_copy(gram_hbm, gram_ref, sems.at[0])
    sample_copy = pltpu.make_async_copy(sample_hbm, sample_ref, sems.at[1])
    gram_copy.start()
    sample_copy.start()
    gram_copy.wait()
    R11, V11 = factor_half(gram_ref[:128], spread.at[0])
    R12 = dot(V11, gram_ref[128:256])
    rest = gram_ref[256:] - dot(R12, R12, 0, 0)
    scale = 1.0 / 256
    sample_copy.wait()
    first = dot(sample_ref[:, :128], V11 * 256.0, 1, 1)
    second = sample_ref[:, 128:] * 256.0 - dot(first, R12)
    basis_ref[:, :128] = first
    tri_ref[:128, :128] = R11 * scale
    tri_ref[:128, 128:] = R12 * scale
    tri_ref[128:, :128] = jnp.zeros((128, 128), jnp.float32)
    R22, V22 = factor_half(rest, spread.at[1])
    tri_ref[128:, 128:] = R22 * scale
    basis_ref[:, 128:] = dot(second, V22, 1, 1)


def chol(gram, values):
    return pl.pallas_call(
        chol_kernel,
        out_shape=(jax.ShapeDtypeStruct((512, 256), jnp.float32), jax.ShapeDtypeStruct((256, 256), jnp.float32)),
        in_specs=[pl.BlockSpec(memory_space=pl.ANY)] * 2,
        out_specs=(pl.BlockSpec(memory_space=pltpu.VMEM),) * 2,
        scratch_shapes=[pltpu.VMEM((384, 128), jnp.float32), pltpu.VMEM((512, 256), jnp.float32), pltpu.VMEM((2, 1280, 128), jnp.float32), pltpu.SemaphoreType.DMA((2,))],
        compiler_params=pltpu.CompilerParams(vmem_limit_bytes=56 << 20),
        name="factor_basis",
    )(gram, values)


def per_device(matrix_blocks, test_panel, column_blocks, row_counts):
    values, gram = sample_and_gram(column_blocks, row_counts, matrix_blocks, test_panel)
    return chol(gram, values)


def solution(mesh):
    in_specs = (P("row", None, None, None), P("row", None), P("row", None), P("row"))
    return jax.shard_map(
        per_device, mesh=mesh, in_specs=in_specs, out_specs=(P("row", None), P()), check_vma=False
    )
```

```python
import functools

import jax
import jax.numpy as jnp
from jax import lax
from jax.experimental import pallas as pl
from jax.experimental.pallas import tpu as pltpu
from jax.sharding import PartitionSpec as P

MESH = pl.DeviceIdType.MESH
HI = lax.Precision.HIGHEST


PIECES = ((0, 160), (160, 176), (336, 176))
HALF = (80, 96, 80)
STEP = (0, 3, 1, 2)
N_COPIES = 180


def sample_kernel(cols_ref, counts_ref, blocks_ref, panel_ref, sample_out, gram_ref, panels, held, sample_ref, table_v, table_s, local, twin_half, terms, send_sem, recv_sem, local_sem, line_send, line_recv, pair_send, pair_recv):
    me = lax.axis_index("row")
    core = me % 2
    coords = [me // 32, (me // 8) % 4, (me // 2) % 4]

    def device(at, which):
        return at[0] * 32 + at[1] * 8 + at[2] * 2 + which

    def shifted(axis, by):
        at = list(coords)
        at[axis] = (at[axis] + by) % 4
        return at

    sibling = device(coords, 1 - core)
    partners = [device(shifted(a, s), core) for a in range(3) for s in (1, 2, 3)] + [sibling]
    barrier = pltpu.get_barrier_semaphore()
    for other in partners:
        pl.semaphore_signal(barrier, inc=1, device_id=(other,), device_id_type=MESH)
    blocks_copy = pltpu.make_async_copy(blocks_ref, held, local_sem.at[0])
    blocks_copy.start()
    own = pltpu.make_async_copy(panel_ref, panels.at[coords[0], coords[1], coords[2], core], local_sem.at[1])
    own.start()
    pl.semaphore_wait(barrier, len(partners))

    started = []
    landed = {}

    def view(where, rows, which=core):
        return panels.at[where[0], where[1], where[2], which, pl.ds(rows[0], rows[1])]

    def push(key, src, dst, target):
        slot = len(started)
        copy = pltpu.make_async_remote_copy(
            src_ref=src, dst_ref=dst, send_sem=send_sem.at[slot], recv_sem=recv_sem.at[slot],
            device_id=(target,), device_id_type=MESH)
        copy.start()
        started.append(copy)
        landed[key] = copy

    def arrive(key):
        landed[key].wait_recv()

    def rows_of(p, part, flip=0):
        first, count = PIECES[p]
        if part is None:
            return (first, count)
        cut = count - HALF[p] if flip else HALF[p]
        return (first, cut) if part == 0 else (first + cut, count - cut)

    def spot(p, ka, kb, kc, among=(0, 4)):
        where = [None] * 3
        for axis, k in ((p, ka), ((p + 1) % 3, kb), ((p + 2) % 3, kc)):
            where[axis] = pl.ds(*among) if k is None else (coords[axis] + STEP[k]) % 4
        return where

    def send(key, p, axis, sign, where, rows, from_panel=False):
        src = panel_ref.at[pl.ds(rows[0], rows[1])] if from_panel else view(where, rows)
        push(key, src, view(where, rows), device(shifted(axis, sign), core))

    def twin(key, p, where, rows):
        push(key, view(where, rows), view(where, rows), sibling)

    PS = range(3)
    for p in PS:
        for k, sign in ((1, 1), (2, 3)):
            send((p, 1, k), p, p, sign, spot(p, 0, 0, 0), rows_of(p, None), True)
    for p in PS:
        for k, sign in ((1, 1), (2, 3)):
            send((p, 2, 0, k), p, (p + 1) % 3, sign, spot(p, 0, 0, 0), rows_of(p, None), True)

    lane = lax.broadcasted_iota(jnp.int32, (8, 128), 1)
    table = jnp.zeros((8, 128), jnp.int32)
    for r in range(2):
        def mark(s, found, r=r):
            column = cols_ref[r, s]
            holder = jnp.where(s < counts_ref[r], column >> 1, -1)
            return jnp.where(lane == holder, 1 + 2 * (r * 48 + s) + (column & 1), found)
        table = lax.fori_loop(0, 48, mark, table)
    table_v[...] = table
    table_copy = pltpu.make_async_copy(table_v, table_s, local_sem.at[2])
    table_copy.start()
    sample_ref[...] = jnp.zeros((512, 256), jnp.float32)

    for ka, sign, part in ((1, 1, 0), (2, 3, 1)):
        for p in PS:
            arrive((p, 1, ka))
            send((p, 1, 3, part), p, p, sign, spot(p, ka, 0, 0), rows_of(p, part, p % 2))
            for k, s in ((1, 1), (2, 3)):
                send((p, 2, ka, k), p, (p + 1) % 3, s, spot(p, ka, 0, 0), rows_of(p, None))
    own.wait()
    table_copy.wait()

    def forward_b(ka):
        for kb, sign, part in ((1, 1, 0), (2, 3, 1)):
            for p in PS:
                arrive((p, 2, ka, kb))
                send((p, 2, ka, 3, part), p, (p + 1) % 3, sign, spot(p, ka, kb, 0), rows_of(p, part, ka % 2))

    def send_c(kb):
        for p in PS:
            for k, s in ((1, 1), (2, 3)):
                send((p, 3, kb, k), p, (p + 2) % 3, s, spot(p, None, kb, 0), rows_of(p, None))
        for p in PS:
            twin((p, 4, kb, 0), p, spot(p, None, kb, 0), rows_of(p, None))

    def cuts(kb):
        return ((0, 2), (2, 2)) if kb == 3 else ((0, 4),)

    def forward_c(kb):
        for kc, sign, part in ((1, 1, 0), (2, 3, 1)):
            for p in PS:
                arrive((p, 3, kb, kc))
                for among in cuts(kb):
                    send((p, 3, kb, 3, part, among), p, (p + 2) % 3, sign, spot(p, None, kb, kc, among), rows_of(p, part, kb % 2))
                twin((p, 4, kb, kc), p, spot(p, None, kb, kc), rows_of(p, None))

    def last_c(kb):
        for among in cuts(kb):
            for p in PS:
                for part in range(2):
                    arrive((p, 3, kb, 3, part, among))
                    twin((p, 4, kb, 3, part, among), p, spot(p, None, kb, 3, among), rows_of(p, part, kb % 2))

    def twins(pairs):
        for kb, kc in pairs:
            for p in PS:
                if kc < 3:
                    arrive((p, 4, kb, kc))
                    continue
                for among in cuts(kb):
                    for part in range(2):
                        arrive((p, 4, kb, 3, part, among))

    def add_products(units):
        tops, bottoms, rights = [], [], []
        for shift, which in units:
            at = [(coords[i] + shift[i]) % 4 for i in range(3)]
            code = table_s[0, device(at, which)]
            index = jnp.maximum(code - 1, 0)
            slot = index >> 1
            block = held[jnp.where(slot >= 48, 1, 0), jnp.where(slot >= 48, slot - 48, slot)]
            none = jnp.zeros_like(block)
            tops.append(jnp.where((code > 0) & (slot < 48), block, none))
            bottoms.append(jnp.where((code > 0) & (slot >= 48), block, none))
            here = panels.at[at[0], at[1], at[2], which]
            rights.append(jnp.where((index & 1) == 0, here[:256], here[256:]))
        left = jnp.concatenate([jnp.concatenate(tops, axis=1), jnp.concatenate(bottoms, axis=1)], axis=0)
        sample_ref[...] += jnp.dot(left, jnp.concatenate(rights, axis=0), preferred_element_type=jnp.float32)

    def near(first, last):
        @pl.loop(first, last)
        def _(i):
            add_products([((i // 3 + 3, i % 3 + 3, k), w) for k in (3, 0, 1) for w in (0, 1)])

    def one_far(kb, which):
        @pl.loop(0, 3)
        def _(i):
            add_products([
                (tuple(jnp.where(axis == i, 2, jnp.where(axis == (i + 2) % 3, STEP[kb], k)) for axis in range(3)), which)
                for k in (3, 0, 1)])

    def more_far(which):
        @pl.loop(0, 2)
        def _(i):
            units = []
            for n in range(5):
                j = 5 * i + n
                axis, u = j // 3, j % 3 + 3
                units.append((tuple(jnp.where(axis == a, u, 2) for a in range(3)), which))
            add_products(units)

    forward_b(0)
    for p in PS:
        arrive((p, 1, 3, 0))
        arrive((p, 1, 3, 1))
        for k, s in ((1, 1), (2, 3)):
            send((p, 2, 3, k), p, (p + 1) % 3, s, spot(p, 3, 0, 0), rows_of(p, None))
    send_c(0)
    forward_b(1)
    forward_b(2)
    forward_b(3)
    send_c(1)
    send_c(2)
    for p in PS:
        for ka in range(4):
            arrive((p, 2, ka, 3, 0))
            arrive((p, 2, ka, 3, 1))
    send_c(3)
    blocks_copy.wait()
    forward_c(0)
    forward_c(1)
    forward_c(2)
    twins([(kb, kc) for kb in range(3) for kc in range(3)])
    near(0, 6)
    forward_c(3)
    near(6, 9)
    last_c(0)
    one_far(0, core)
    last_c(1)
    twins([(3, kc) for kc in range(3)] + [(0, 3)])
    one_far(0, 1 - core)
    one_far(1, core)
    last_c(2)
    twins([(1, 3)])
    one_far(1, 1 - core)
    one_far(2, core)
    last_c(3)
    twins([(2, 3)])
    one_far(2, 1 - core)
    more_far(core)
    twins([(3, 3)])
    more_far(1 - core)

    sample_copy = pltpu.make_async_copy(sample_ref, sample_out, local_sem.at[3])
    sample_copy.start()
    v = sample_ref[...]
    gram = lax.dot_general(v, v, (((0,), (0,)), ((), ())), precision=HI, preferred_element_type=jnp.float32)
    local[:128] = gram[:128, :128]
    local[128:256] = gram[:128, 128:]
    local[256:] = gram[128:, 128:]

    def part_rows(which, q):
        return pl.ds(pl.multiple_of(which * 192 + 64 * q, 64), 64)

    pairs, lines, backs = [], {}, []
    for q in PS:
        pairs.append(pltpu.make_async_remote_copy(
            src_ref=local.at[part_rows(1 - core, q)], dst_ref=twin_half.at[q], send_sem=pair_send.at[0, q], recv_sem=pair_recv.at[0, q],
            device_id=(sibling,), device_id_type=MESH))
        pairs[q].start()

    def along(t, q, value):
        axis = (q + t) % 3
        mine = terms.at[t, q, coords[axis]]
        mine[...] = value
        for i in (2, 1, 3):
            copy = pltpu.make_async_remote_copy(
                src_ref=mine, dst_ref=mine, send_sem=line_send.at[t, q, i - 1], recv_sem=line_recv.at[t, q, i - 1],
                device_id=(device(shifted(axis, i), core),), device_id_type=MESH)
            copy.start()
            lines[t, q, i] = copy

    for q in PS:
        pairs[q].wait_recv()
        along(0, q, local[part_rows(core, q)] + twin_half[q])
    for copy in started + pairs:
        copy.wait_send()
    sample_copy.wait()
    for t in range(3):
        if t:
            for q in PS:
                for i in (1, 3, 2):
                    lines[t - 1, q, i].wait_send()
        for q in PS:
            for i in (1, 3, 2):
                lines[t, q, i].wait_recv()
            total = (terms[t, q, 0] + terms[t, q, 1]) + (terms[t, q, 2] + terms[t, q, 3])
            if t < 2:
                along(t + 1, q, total)
                continue
            twin_half[q] = total
            backs.append(pltpu.make_async_copy(twin_half.at[q], gram_ref.at[part_rows(core, q)], local_sem.at[4 + q]))
            backs[-1].start()
            backs.append(pltpu.make_async_remote_copy(
                src_ref=twin_half.at[q], dst_ref=gram_ref.at[part_rows(core, q)], send_sem=pair_send.at[1, q], recv_sem=pair_recv.at[1, q],
                device_id=(sibling,), device_id_type=MESH))
            backs[-1].start()
    for q in PS:
        for i in (1, 3, 2):
            lines[2, q, i].wait_send()
    for copy in backs:
        copy.wait()
    assert len(started) == N_COPIES, len(started)


def sample_and_gram(cols, counts, blocks, panel):
    return pl.pallas_call(
        sample_kernel,
        out_shape=(jax.ShapeDtypeStruct((512, 256), jnp.float32), jax.ShapeDtypeStruct((384, 128), jnp.float32)),
        in_specs=[pl.BlockSpec(memory_space=pltpu.SMEM)] * 2 + [pl.BlockSpec(memory_space=pl.ANY)] * 2,
        out_specs=(pl.BlockSpec(memory_space=pl.ANY),) * 2,
        scratch_shapes=[
            pltpu.VMEM((4, 4, 4, 2, 512, 256), jnp.bfloat16),
            pltpu.VMEM((2, 48, 256, 256), jnp.bfloat16),
            pltpu.VMEM((512, 256), jnp.float32),
            pltpu.VMEM((8, 128), jnp.int32),
            pltpu.SMEM((8, 128), jnp.int32),
            pltpu.VMEM((384, 128), jnp.float32),
            pltpu.VMEM((3, 64, 128), jnp.float32),
            pltpu.VMEM((3, 3, 4, 64, 128), jnp.float32),
            pltpu.SemaphoreType.DMA((N_COPIES,)),
            pltpu.SemaphoreType.DMA((N_COPIES,)),
            pltpu.SemaphoreType.DMA((7,)),
            pltpu.SemaphoreType.DMA((3, 3, 3)),
            pltpu.SemaphoreType.DMA((3, 3, 3)),
            pltpu.SemaphoreType.DMA((2, 3)),
            pltpu.SemaphoreType.DMA((2, 3)),
        ],
        compiler_params=pltpu.CompilerParams(collective_id=0, has_side_effects=True, vmem_limit_bytes=56 << 20),
        name="sample_gram",
    )(cols, counts, blocks, panel)


def dot(a, b, ca=1, cb=0):
    return lax.dot_general(a, b, (((ca,), (cb,)), ((), ())), precision=HI, preferred_element_type=jnp.float32)


def factor_half(s, spread, n=128):
    tiles = n // 8
    sub = lax.broadcasted_iota(jnp.int32, (8, n), 0)
    lane = lax.broadcasted_iota(jnp.int32, (8, n), 1)
    S = [s[8 * i:8 * i + 8] for i in range(tiles)]
    W = [jnp.where(lane == sub + 8 * i, 1.0, 0.0).astype(jnp.float32) for i in range(tiles)]

    def row(place, i):
        return spread[pl.ds(8 * place + i, 8, stride=0), :]

    def put(place, x):
        spread[8 * place:8 * place + 8, :] = x

    def column(x, j):
        return jnp.broadcast_to(x[:, j:j + 1], (8, n))

    for k in range(tiles):
        cols = [column(S[k], 8 * k + j) for j in range(8)]
        for j in range(8):
            put(10 * k + j, cols[j])
        put(10 * k + 8, S[k])
        put(10 * k + 9, W[k])
        e = {(i, j): row(10 * k + j, i) for j in range(8) for i in range(j + 1)}
        r = [row(10 * k + 8, i) for i in range(8)]
        w = [row(10 * k + 9, i) for i in range(8)]
        inv, g, ahead = {}, {}, {}
        follow = k + 1 < tiles
        side = [column(S[k + 1], 8 * k + q) for q in range(8)] if follow else None
        kept = list(side) if follow else None
        for j in range(0, 8, 2):
            a, b, c = e[j, j], e[j, j + 1], e[j + 1, j + 1]
            det = a * c - b * b
            inv[j] = pl.reciprocal(det, approx=True)
            ahead[j] = c * r[j] - b * r[j + 1], a * r[j + 1] - b * r[j], c * w[j] - b * w[j + 1], a * w[j + 1] - b * w[j]
            if follow:
                S[k + 1] = S[k + 1] - ((side[j] * ahead[j][0] + side[j + 1] * ahead[j][1]) * inv[j])
            for i in range(j + 2, 8):
                x, y = e[j, i], e[j + 1, i]
                n0, n1 = c * x - b * y, a * y - b * x
                for q in range(i, 8):
                    e[i, q] = e[i, q] - ((n0 * e[j, q] + n1 * e[j + 1, q]) * inv[j])
                g[i, j], g[i, j + 1] = n0 * inv[j], n1 * inv[j]
                if follow:
                    side[i] = side[i] - (g[i, j] * side[j] + g[i, j + 1] * side[j + 1])
                r[i] = r[i] - (g[i, j] * r[j] + g[i, j + 1] * r[j + 1])
                w[i] = w[i] - (g[i, j] * w[j] + g[i, j + 1] * w[j + 1])
        if k + 1 < tiles:
            t, u = [None] * 8, [None] * 8
            for j in (6, 4, 2, 0):
                t[j], t[j + 1], u[j], u[j + 1] = [v * inv[j] for v in ahead[j]]
                for m in range(j + 2, 8, 2):
                    for h in (j, j + 1):
                        t[h] = t[h] - (g[m, h] * t[m] + g[m + 1, h] * t[m + 1])
                        u[h] = u[h] - (g[m, h] * u[m] + g[m + 1, h] * u[m + 1])
            for i in range(k + 1, tiles):
                c = kept if i == k + 1 else [column(S[i], 8 * k + q) for q in range(8)]
                S[i] = S[i] if i == k + 1 else ((S[i] - (c[6] * t[6] + c[7] * t[7])) - (c[4] * t[4] + c[5] * t[5])) - (c[2] * t[2] + c[3] * t[3]) - (c[0] * t[0] + c[1] * t[1])
                W[i] = ((W[i] - (c[6] * u[6] + c[7] * u[7])) - (c[4] * u[4] + c[5] * u[5])) - (c[2] * u[2] + c[3] * u[3]) - (c[0] * u[0] + c[1] * u[1])
        for j in range(0, 8, 2):
            slope = e[j, j + 1] * pl.reciprocal(e[j, j], approx=True)
            r[j + 1] = r[j + 1] - slope * r[j]
            w[j + 1] = w[j + 1] - slope * w[j]
            e[j + 1, j + 1] = e[j + 1, j + 1] - slope * e[j, j + 1]
        new_s, new_w = r[0], w[0]
        d = e[0, 0]
        for i in range(1, 8):
            new_s = jnp.where(sub == i, r[i], new_s)
            new_w = jnp.where(sub == i, w[i], new_w)
            d = jnp.where(sub == i, e[i, i], d)
        q = lax.rsqrt(d)
        S[k] = jnp.where(lane >= sub + 8 * k, new_s * q, 0.0)
        W[k] = new_w * q
    return jnp.concatenate(S, axis=0), jnp.concatenate(W, axis=0)


def chol_kernel(gram_hbm, sample_hbm, basis_ref, tri_ref, gram_ref, sample_ref, spread, sems):
    gram_copy = pltpu.make_async_copy(gram_hbm, gram_ref, sems.at[0])
    sample_copy = pltpu.make_async_copy(sample_hbm, sample_ref, sems.at[1])
    gram_copy.start()
    sample_copy.start()
    gram_copy.wait()
    R11, V11 = factor_half(gram_ref[:128], spread.at[0])
    R12 = dot(V11, gram_ref[128:256])
    rest = gram_ref[256:] - dot(R12, R12, 0, 0)
    scale = 1.0 / 256
    sample_copy.wait()
    first = dot(sample_ref[:, :128], V11 * 256.0, 1, 1)
    second = sample_ref[:, 128:] * 256.0 - dot(first, R12)
    basis_ref[:, :128] = first
    tri_ref[:128, :128] = R11 * scale
    tri_ref[:128, 128:] = R12 * scale
    tri_ref[128:, :128] = jnp.zeros((128, 128), jnp.float32)
    R22, V22 = factor_half(rest, spread.at[1])
    tri_ref[128:, 128:] = R22 * scale
    basis_ref[:, 128:] = dot(second, V22, 1, 1)


def chol(gram, values):
    return pl.pallas_call(
        chol_kernel,
        out_shape=(jax.ShapeDtypeStruct((512, 256), jnp.float32), jax.ShapeDtypeStruct((256, 256), jnp.float32)),
        in_specs=[pl.BlockSpec(memory_space=pl.ANY)] * 2,
        out_specs=(pl.BlockSpec(memory_space=pltpu.VMEM),) * 2,
        scratch_shapes=[pltpu.VMEM((384, 128), jnp.float32), pltpu.VMEM((512, 256), jnp.float32), pltpu.VMEM((2, 1280, 128), jnp.float32), pltpu.SemaphoreType.DMA((2,))],
        compiler_params=pltpu.CompilerParams(vmem_limit_bytes=56 << 20),
        name="factor_basis",
    )(gram, values)


def per_device(matrix_blocks, test_panel, column_blocks, row_counts):
    values, gram = sample_and_gram(column_blocks, row_counts, matrix_blocks, test_panel)
    return chol(gram, values)


def solution(mesh):
    in_specs = (P("row", None, None, None), P("row", None), P("row", None), P("row"))
    return jax.shard_map(
        per_device, mesh=mesh, in_specs=in_specs, out_specs=(P("row", None), P()), check_vma=False
    )
```
